128 devices in a mesh: pipe: 8 (over y, core), expert: 16 (over x, z).
Axes of the slice: x: 4, y: 4, z: 4, core: 2. Of those that a mesh axis runs over, the one named last changes fastest.
Arguments:
- upstream_first: bfloat16 [8, 2048, 7168], P('pipe', 'expert'), may hold values from -6 to 6
- upstream_last: bfloat16 [2048, 7168], P('expert'), may hold values from -6 to 6
- saved_input: bfloat16 [8, 2, 2048, 7168], P('pipe', None, 'expert'), may hold values from -64 to 64
- norm_gain: float32 [8, 7168], P('pipe'), may hold values from 0.5 to 1.5
- router_weight: float32 [8, 7168, 4], P('pipe'), may hold values from -0.0625 to 0.0625
- routes: int32 [8, 2, 2048, 2], P('pipe', None, 'expert'), may hold values from 0 to 3, all different within a row; in each aligned block of 128 rows (0 to 127, 128 to 255, ..., all dimensions but the last counted through in order) at most 72 rows name the same one
- w_gate: bfloat16 [8, 16, 1792, 1024], P('pipe', 'expert'), may hold values from -0.0625 to 0.0625
- w_up: bfloat16 [8, 16, 1792, 1024], P('pipe', 'expert'), may hold values from -0.0625 to 0.0625
- w_down: bfloat16 [8, 16, 1024, 1792], P('pipe', 'expert'), may hold values from -0.1875 to 0.1875
- saved_preact: bfloat16 [8, 2, 16, 288, 2048], P('pipe', None, 'expert'), may hold values from -6 to 6
Outputs:
- grad_first: bfloat16 [8, 2048, 7168], P('pipe', 'expert')
- grad_second: bfloat16 [8, 2048, 7168], P('pipe', 'expert')
The draws below stay inside these ranges and needn't reach their ends.
Inputs may be any that keep to these rules, and one draw needn't show every extreme that they name: `routes`: each row names 2 different experts. Within the rows of one device of one section and wave, no expert is named by more than 72 rows, a bound that some block reaches.
All inputs are finite; a program needn't handle non-finite values.
Results may differ from the reference program's by a relative error of at most 0.011.
Values may be sent and summed in bfloat16 or wider, within the bound.
No kernel may reach another device: no remote copies, remote signals or barrier semaphores. Data moves between devices by JAX's collectives and lax.ppermute only.
A program may use at most 128 MiB of HBM per device.

```python
import math
import jax
import jax.numpy as jnp
import numpy as np
from jax import lax

D = 7168
HID = 1024
EXPERTS = 4
TOP = 2
TOK_DEV = 128
CAP = 72
DPART = 1792
SHARE = 288
TOKENS = 2048
SECTIONS = 8
N_EXPERT = 16


def draw_saved_input(key, part):
    key = jax.random.fold_in(key, 11)
    first_key, row_key, col_key = jax.random.split(key, 3)
    shape = (SECTIONS, 2, TOKENS, D)
    base = jnp.clip(jax.random.normal(first_key, shape, jnp.float32), -4.0, 4.0)
    row_scale = jnp.exp(jax.random.uniform(row_key, (SECTIONS, 2, TOKENS, 1), jnp.float32, -1.2, 1.2))
    col_scale = jnp.exp(jax.random.uniform(col_key, (1, 1, 1, D), jnp.float32, -1.2, 1.2))
    return (base * row_scale * col_scale).astype(jnp.bfloat16)


def shard_levels(stream_key, shape, cuts, low, high):
    loudness, own = 1.0, jax.random.fold_in(stream_key, 6)
    for axis_at, parts in cuts:
        heights = jnp.exp(jax.random.uniform(jax.random.fold_in(own, axis_at), (parts,), jnp.float32, low / len(cuts), high / len(cuts)))
        loudness = loudness * jnp.repeat(heights, shape[axis_at] // parts).reshape([-1 if axis == axis_at else 1 for axis in range(len(shape))])
    return loudness


def routed_block(stream_key, own, number, rows, number_of, top, reach, slope):
    order = jax.random.permutation(stream_key, number_of)
    heavy_load, usual = shares(number_of, rows * top, reach, slope, True), shares(number_of, rows * top, reach, slope, False)
    places = jnp.arange(number_of)

    def named(sizes, turn):
        used = int((sizes > 0).sum())
        fixed = max(1, used // 4)
        passed = fixed + (places - fixed + turn * (used - fixed)) % max(1, number_of - fixed)
        return jnp.zeros((number_of,), jnp.int32).at[order[jnp.where(places < fixed, places, passed)]].set(jnp.asarray(sizes, jnp.int32))

    sizes = jnp.where(number % 4 == 0, named(heavy_load, number // 4), named(usual, number - number // 4 - 1))
    mixed = jax.random.permutation(jax.random.fold_in(own, 3), number_of)
    donor, taker = mixed[0:number_of // 2 * 2:2], mixed[1:number_of // 2 * 2:2]
    slack = jnp.minimum(sizes[donor] - 1, reach - sizes[taker]) // 2
    slack = jnp.where((donor == order[0]) | (taker == order[0]) | (sizes[taker] == 0), 0, jnp.maximum(slack, 0))
    passed = jax.random.randint(jax.random.fold_in(own, 4), (number_of // 2,), 0, 1 << 20) % (slack + 1)
    sizes = sizes.at[donor].add(-passed).at[taker].add(passed)
    members = jnp.searchsorted(jnp.cumsum(sizes), jnp.arange(rows * top), side="right").astype(jnp.int32)
    grid = members.reshape(top, rows).T
    grid = grid[jax.random.permutation(jax.random.fold_in(own, 1), rows)]
    turn = jax.random.randint(jax.random.fold_in(own, 2), (rows, 1), 0, top)
    return jnp.take_along_axis(grid, (jnp.arange(top)[None, :] + turn) % top, axis=1)


def shares(number_of, total, bound, lean, full):
    portions = [(1 << 20) // math.isqrt(grade ** lean) + 1 for grade in range(1, number_of + 1)]
    largest = bound if full else min(bound, max(-(-total // number_of), total * portions[0] // sum(portions)))
    least = 1 if total - largest >= number_of - 1 else 0
    counts, spare = [largest] + [least] * (number_of - 1), total - largest - least * (number_of - 1)
    while spare > 0:
        movable = [i for i in range(1, number_of) if counts[i] < largest] or [i for i in range(1, number_of) if counts[i] < bound]
        mass, left = sum([portions[i] for i in movable]), spare
        for i in movable:
            addition = min(bound - counts[i], max(1, left * portions[i] // mass), spare)
            counts[i] = counts[i] + addition
            spare = spare - addition
    return np.array(counts)


def centred(own_key, extent, width, most, shards=(), held_as=jnp.bfloat16):
    factor_of = shard_levels(own_key, extent, shards, -0.22, 0.18) if shards else 1.0
    entries = jax.random.normal(own_key, extent, jnp.float32) * width * factor_of
    return jnp.minimum(jnp.maximum(entries, -most), most).astype(held_as)


def setup_inputs(seed: int = 0) -> dict:
    splits = jax.random.split(jax.random.key(seed), 11)
    upstream_first = centred(splits[0], (SECTIONS, TOKENS, D), 1.0, 6.0, ((0, 8), (1, 16)))
    upstream_last = centred(splits[1], (TOKENS, D), 1.0, 6.0, ((0, 16),))
    saved_input = draw_saved_input(jax.random.fold_in(splits[10], 71), 0)
    norm_gain = jnp.clip(1.0 + 0.1 * jax.random.normal(splits[3], (SECTIONS, D), jnp.float32), 0.5, 1.5)
    router_weight = centred(splits[4], (SECTIONS, D, EXPERTS), D ** -0.5, 0.0625, ((0, 8),), jnp.float32)
    routes_keys = jax.random.split(jax.random.fold_in(splits[5], 1), SECTIONS * 2 * TOKENS // TOK_DEV)
    routes_turns = jax.random.permutation(jax.random.fold_in(splits[5], 3), SECTIONS * 2 * TOKENS // TOK_DEV)
    routes = jax.vmap(lambda own, number: routed_block(jax.random.fold_in(splits[5], 2), own, number, TOK_DEV, EXPERTS, TOP, CAP, 2))(routes_keys, routes_turns).reshape((SECTIONS, 2, TOKENS, TOP))
    w_gate = centred(splits[6], (SECTIONS, N_EXPERT, DPART, HID), D ** -0.5, 0.0625, ((0, 8), (1, 16)))
    w_up = centred(splits[7], (SECTIONS, N_EXPERT, DPART, HID), D ** -0.5, 0.0625, ((0, 8), (1, 16)))
    w_down = centred(splits[8], (SECTIONS, N_EXPERT, HID, DPART), HID ** -0.5, 0.1875, ((0, 8), (1, 16)))
    saved_preact = centred(splits[9], (SECTIONS, 2, N_EXPERT, SHARE, 2 * HID), 1.0, 6.0, ((0, 8), (2, 16)))
    return dict(upstream_first=upstream_first, upstream_last=upstream_last, saved_input=saved_input, norm_gain=norm_gain, router_weight=router_weight, routes=routes, w_gate=w_gate, w_up=w_up, w_down=w_down, saved_preact=saved_preact)


epsilon = 1e-06
route_scale = 2.5

def section(upstream, saved_rows, gain, router, routing, w_gate, w_up, w_down, preact):
    split_count = N_EXPERT // EXPERTS
    part_width = D // split_count
    slot_total = N_EXPERT * CAP
    inputs = saved_rows.astype(jnp.float32)
    inverse = lax.rsqrt(lax.optimization_barrier(jnp.mean(inputs * inputs, axis=-1, keepdims=True)) + epsilon)
    normed = inputs * inverse * gain
    logits = jnp.dot(normed, router, precision=lax.Precision.HIGHEST, preferred_element_type=jnp.float32)
    affinity = jax.nn.sigmoid(logits)
    chosen = jnp.take_along_axis(affinity, routing, axis=1)
    total_sum = lax.optimization_barrier(jnp.sum(chosen, axis=-1, keepdims=True))
    weights = route_scale * chosen / total_sum
    expert_flat = routing.reshape(-1).astype(jnp.int32)
    onehot = (expert_flat.reshape(N_EXPERT, TOK_DEV * TOP)[:, :, None] == jnp.arange(EXPERTS, dtype=jnp.int32)).astype(jnp.int32)
    ranking = lax.optimization_barrier(jnp.sum(onehot * (jnp.cumsum(onehot, axis=1) - 1), axis=-1)).reshape(-1).astype(jnp.int32)
    pair_index = jnp.arange(TOKENS * TOP, dtype=jnp.int32)
    slot_rows = expert_flat * slot_total + pair_index // (TOK_DEV * TOP) * CAP + ranking
    token_index = pair_index // TOP
    buffers = jnp.zeros((EXPERTS * slot_total, D), jnp.bfloat16).at[slot_rows].set(upstream[token_index])
    buffers = buffers.reshape(EXPERTS, slot_total, D)
    gate_full = w_gate.reshape(EXPERTS, D, HID)
    up_full = w_up.reshape(EXPERTS, D, HID)
    down_full = w_down.reshape(EXPERTS, split_count, HID, part_width)
    acts = preact.reshape(EXPERTS, slot_total, 2 * HID)

    def per_expert(items):
        rows, gate_w, up_w, down_w, act = items
        pieces = rows.reshape(slot_total, split_count, part_width).astype(jnp.float32)
        partial_value = jnp.einsum('rqd,qhd->qrh', pieces, down_w.astype(jnp.float32))
        partial_value = lax.optimization_barrier(partial_value.astype(jnp.bfloat16)).astype(jnp.float32)
        hidden_grad = lax.optimization_barrier(jnp.sum(partial_value, axis=0))
        gate_pre = act[:, :HID].astype(jnp.float32)
        up_pre = act[:, HID:].astype(jnp.float32)
        sigmoid_g = jax.nn.sigmoid(gate_pre)
        silu_g = gate_pre * sigmoid_g
        score_grad = lax.optimization_barrier(jnp.sum(hidden_grad * silu_g * up_pre, axis=-1)).astype(jnp.bfloat16)
        gate_grad = (hidden_grad * up_pre * sigmoid_g * (1.0 + gate_pre * (1.0 - sigmoid_g))).astype(jnp.bfloat16)
        up_grad = (hidden_grad * silu_g).astype(jnp.bfloat16)
        back_rows = jnp.dot(gate_grad, gate_w.T, preferred_element_type=jnp.float32)
        back_rows = back_rows + jnp.dot(up_grad, up_w.T, preferred_element_type=jnp.float32)
        return (back_rows.astype(jnp.bfloat16), score_grad)
    backs, scores = lax.map(per_expert, (buffers, gate_full, up_full, down_full, acts))
    back_flat = backs.reshape(EXPERTS * slot_total, D)
    picked = back_flat[slot_rows].astype(jnp.float32).reshape(TOKENS, TOP, D)
    score_pick = scores.reshape(-1)[slot_rows].astype(jnp.float32).reshape(TOKENS, TOP)
    normed_grad = lax.optimization_barrier(jnp.sum(weights[:, :, None] * picked, axis=1))
    mixed = lax.optimization_barrier(jnp.sum(score_pick * chosen, axis=-1, keepdims=True)) / total_sum
    chosen_grad = route_scale * (score_pick - mixed) / total_sum
    logit_pair = chosen_grad * chosen * (1.0 - chosen)
    columns = (routing[:, :, None] == jnp.arange(EXPERTS, dtype=jnp.int32)).astype(jnp.float32)
    dense_grad = lax.optimization_barrier(jnp.sum(logit_pair[:, :, None] * columns, axis=1))
    normed_grad = normed_grad + jnp.dot(dense_grad, router.T, precision=lax.Precision.HIGHEST, preferred_element_type=jnp.float32)
    gained = normed_grad * gain
    input_grad = inverse * gained - inputs * inverse ** 3 * lax.optimization_barrier(jnp.mean(inputs * gained, axis=-1, keepdims=True))
    return (upstream.astype(jnp.float32) + input_grad).astype(jnp.bfloat16)

def reference(upstream_first, upstream_last, saved_input, norm_gain, router_weight, routes, w_gate, w_up, w_down, saved_preact):
    firsts = []
    for section_num in range(SECTIONS):
        firsts.append(section(upstream_first[section_num], saved_input[section_num, 0], norm_gain[section_num], router_weight[section_num], routes[section_num, 0], w_gate[section_num], w_up[section_num], w_down[section_num], saved_preact[section_num, 0]))
    seconds = []
    for section_num in range(SECTIONS):
        if section_num + 1 < SECTIONS:
            upstream = firsts[section_num + 1]
        else:
            upstream = upstream_last
        seconds.append(section(upstream, saved_input[section_num, 1], norm_gain[section_num], router_weight[section_num], routes[section_num, 1], w_gate[section_num], w_up[section_num], w_down[section_num], saved_preact[section_num, 1]))
    return (jnp.stack(firsts), jnp.stack(seconds))
```

```python
import jax
import jax.numpy as jnp
from jax import lax
from jax.sharding import Mesh
from jax.sharding import PartitionSpec as P

CAP = 72
EXPERTS = 4
CHUNKS = ((0, 1), (2, 3))

epsilon = 1e-06
route_scale = 2.5


def turned(value, axis, offset):
    if offset == 0:
        return value
    count = lax.axis_size(axis)
    return lax.ppermute(value, axis, [(i, (i + offset) % count) for i in range(count)])


def pick(stacked, index):
    return lax.dynamic_index_in_dim(stacked, index, 0, keepdims=False)


def split_in_two(value):
    high = value.astype(jnp.bfloat16)
    return high, (value - high.astype(jnp.float32)).astype(jnp.bfloat16)


def token_values(saved_input, gain, router, routes):
    waves, tokens, width = saved_input.shape
    flat = saved_input.reshape(waves * tokens, width)
    inputs = flat.astype(jnp.float32)
    inverse = lax.rsqrt(jnp.mean(inputs * inputs, axis=-1) + epsilon)
    scaled = gain[:, None] * router
    high = scaled.astype(jnp.bfloat16)
    rest = scaled - high.astype(jnp.float32)
    middle = rest.astype(jnp.bfloat16)
    low = (rest - middle.astype(jnp.float32)).astype(jnp.bfloat16)
    parts = jnp.dot(
        flat, jnp.concatenate([high, middle, low], axis=1), preferred_element_type=jnp.float32
    ).reshape(waves * tokens, 3, EXPERTS)
    logits = (parts[:, 0] + (parts[:, 1] + parts[:, 2])) * inverse[:, None]
    affinity = jax.nn.sigmoid(logits).reshape(waves, tokens, EXPERTS)
    routed = (routes[..., None] == jnp.arange(EXPERTS, dtype=jnp.int32)).astype(jnp.float32)
    chosen = jnp.sum(routed * affinity[:, :, None, :], axis=-1)
    total = jnp.sum(chosen, axis=-1, keepdims=True)
    weights = route_scale * chosen / total
    own = (1.0 - chosen) * (1.0 - chosen / total)
    other = -(chosen * (1.0 - chosen) / total)[:, :, ::-1]
    spread = own[..., None] * routed + other[..., None] * routed[:, :, ::-1]
    names = routes.reshape(waves, -1)
    count = names.shape[1]
    places = jnp.arange(count, dtype=jnp.int32)
    earlier = (names[:, :, None] == names[:, None, :]) & (places[None, :] < places[:, None])
    rank = jnp.sum(earlier.astype(jnp.int32), axis=-1)
    slots = (names * CAP + rank).reshape(waves, tokens, 2).astype(jnp.float32)
    packed = jnp.concatenate(
        [
            slots,
            weights,
            inverse.reshape(waves, tokens, 1),
            spread.reshape(waves, tokens, 2 * EXPERTS),
            jnp.zeros((waves, tokens, 3), jnp.float32),
        ],
        axis=-1,
    )
    return inverse.reshape(waves, tokens), jnp.swapaxes(packed, 1, 2)


def on_device(
    upstream_first,
    upstream_last,
    saved_input,
    norm_gain,
    router_weight,
    routes,
    w_gate,
    w_up,
    w_down,
    saved_preact,
):
    side = lax.axis_size("z")
    x_at, z_at = lax.axis_index("x"), lax.axis_index("z")
    pipe_count = lax.axis_size("pipe")
    is_last = lax.axis_index("pipe") == pipe_count - 1
    upstream_first, saved_input = upstream_first[0], saved_input[0]
    gain, router, routes = norm_gain[0], router_weight[0], routes[0]
    down_cols, preact = w_down[0, 0], saved_preact[0, :, 0]
    tokens, width = upstream_first.shape
    part = width // side
    hidden = down_cols.shape[0]

    def feature_block(value, index):
        return lax.dynamic_slice_in_dim(value, index % side * part, part, value.ndim - 1)

    def by_source(blocks):
        stacked = jnp.stack(blocks)
        return [pick(stacked, (z_at - source) % side) for source in range(side)]

    def spread_features(value):
        return by_source(
            [turned(feature_block(value, z_at + off), "z", off) for off in range(side)]
        )

    def gather_features(blocks):
        stacked = jnp.stack(blocks)
        got = jnp.stack(
            [turned(pick(stacked, (z_at + off) % side), "z", off) for off in range(side)]
        )
        return jnp.concatenate([pick(got, (z_at - q) % side) for q in range(side)], axis=1)

    def pipe_back(value):
        return lax.ppermute(value, "pipe", [(i, i - 1) for i in range(1, pipe_count)])

    first_blocks = spread_features(upstream_first)
    inverse, packed = token_values(saved_input, gain, router, routes)
    facts = jnp.stack(by_source([turned(packed, "z", off) for off in range(side)]))
    input_blocks = spread_features(saved_input[0])
    last_blocks = []
    for off in range(side):
        value = feature_block(upstream_last, z_at + off)
        if off:
            stage = pipe_count - 1
            value = lax.ppermute(
                value,
                ("pipe", "z"),
                [(stage * side + i, stage * side + (i + off) % side) for i in range(side)],
            )
        last_blocks.append(value)
    last_blocks = by_source(last_blocks)

    gain_block = feature_block(gain, z_at)
    router_block = lax.dynamic_slice_in_dim(router, z_at * part, part, 0)
    router_high, router_low = split_in_two(router_block)
    back_weight = jnp.concatenate(
        [
            w_gate[0, 0],
            w_up[0, 0],
            router_high,
            router_high,
            router_low,
            jnp.zeros((part, 128 - 3 * EXPERTS), jnp.bfloat16),
        ],
        axis=1,
    )

    rows = jnp.arange(CAP, dtype=jnp.int32)[:, None]

    def matches(wave, source, expert, k):
        place = facts[source, wave, k].astype(jnp.int32) - expert * CAP
        return place[None, :] == rows

    def placing(wave, source, off):
        expert = (x_at + off) % side
        both = matches(wave, source, expert, 0) | matches(wave, source, expert, 1)
        return both.astype(jnp.bfloat16)

    def weighing(wave, source, off):
        expert = (x_at - off) % side
        value = sum(
            jnp.where(matches(wave, source, expert, k), facts[source, wave, 2 + k][None, :], 0.0)
            for k in range(2)
        )
        return value.astype(jnp.bfloat16)

    def slot_spread(off):
        expert = (x_at + off) % side
        value = 0.0
        for k in range(2):
            match = jnp.stack(
                [
                    jnp.stack([matches(wave, source, expert, k) for source in range(side)])
                    for wave in range(2)
                ]
            ).astype(jnp.float32)
            fact = jnp.swapaxes(facts[:, :, 5 + 4 * k : 9 + 4 * k], 0, 1)
            value = value + jnp.einsum("wsrt,wsat->wsra", match, fact, precision="highest")
        return turned(value.reshape(2, side * CAP, EXPERTS), "x", off)

    spreads = pick(jnp.stack([slot_spread(off) for off in range(side)]), (x_at - z_at) % side)

    def experts_of(wave, sources, blocks):
        depth = len(sources) * CAP
        upstream = jnp.stack(blocks)
        arrived = {}
        for off in (2, 1, 3, 0):
            place = jnp.stack([placing(wave, source, off) for source in sources])
            sent = jnp.einsum(
                "srt,stf->srf", place, upstream, preferred_element_type=jnp.bfloat16
            ).reshape(depth, part)
            arrived[off] = turned(sent, "x", off)
        arrived = jnp.concatenate([arrived[off] for off in range(side)])
        partial = lax.dot_general(
            arrived, down_cols, (((1,), (1,)), ((), ())), preferred_element_type=jnp.float32
        ).astype(jnp.bfloat16).reshape(side, depth, hidden)
        pieces = [pick(partial, (x_at - z_at - off) % side) for off in range(side)]
        half = hidden // 2
        upward = turned(pieces[2][:, :half], "z", 1)
        downward = turned(pieces[2][:, half:], "z", -1)
        f32 = jnp.float32
        up_sum = jnp.concatenate(
            [(pieces[1][:, :half].astype(f32) + upward.astype(f32)).astype(jnp.bfloat16), pieces[1][:, half:]],
            axis=1,
        )
        down_sum = jnp.concatenate(
            [pieces[3][:, :half], (pieces[3][:, half:].astype(f32) + downward.astype(f32)).astype(jnp.bfloat16)],
            axis=1,
        )
        hidden_grad = (
            pieces[0].astype(f32)
            + turned(up_sum, "z", 1).astype(f32)
            + turned(down_sum, "z", -1).astype(f32)
        )
        start = sources[0] * CAP
        acts = preact[wave, start : start + depth]
        gate_pre = acts[:, :hidden].astype(f32)
        up_pre = acts[:, hidden:].astype(f32)
        sigmoid_g = jax.nn.sigmoid(gate_pre)
        silu_g = gate_pre * sigmoid_g
        score = jnp.sum(hidden_grad * silu_g * up_pre, axis=-1).astype(jnp.bfloat16).astype(f32)
        gate_grad = hidden_grad * up_pre * sigmoid_g * (1.0 + gate_pre * (1.0 - sigmoid_g))
        up_grad = hidden_grad * silu_g
        score_high, score_low = split_in_two(score[:, None] * spreads[wave, start : start + depth])
        grads = jnp.concatenate(
            [
                gate_grad.astype(jnp.bfloat16),
                up_grad.astype(jnp.bfloat16),
                score_high,
                score_low,
                score_high,
                jnp.zeros((depth, 128 - 3 * EXPERTS), jnp.bfloat16),
            ],
            axis=1,
        )
        from_below = turned(grads, "z", 1)
        from_above = turned(grads, "z", -1)
        far = [turned(from_below[: depth // 2], "z", 1), turned(from_above[depth // 2 :], "z", -1)]
        gathered = jnp.concatenate([grads, from_above] + far + [from_below])
        back = lax.dot_general(
            gathered, back_weight, (((1,), (1,)), ((), ())), preferred_element_type=jnp.float32
        ).astype(jnp.bfloat16).reshape(side, depth, part)
        normed_grad = 0.0
        for off in (2, 1, 3, 0):
            returned = turned(pick(back, (x_at + off - z_at) % side), "x", off)
            weigh = jnp.stack([weighing(wave, source, off) for source in sources])
            normed_grad = normed_grad + jnp.einsum(
                "srt,srf->stf",
                weigh,
                returned.reshape(len(sources), CAP, part),
                preferred_element_type=f32,
            )
        return normed_grad

    second_blocks, first_out = [None] * side, [None] * side
    for sources in CHUNKS:
        blocks = [first_blocks[source] for source in sources]
        normed_grad = experts_of(0, sources, blocks)
        gained = normed_grad * gain_block
        inputs = jnp.stack([input_blocks[source] for source in sources]).astype(jnp.float32)
        factor = jnp.stack([facts[source, 0, 4] for source in sources])
        share = jnp.sum(inputs * gained, axis=-1)
        mean = sum(turned(share, "z", off) for off in range(side)) / width
        grad = (
            jnp.stack(blocks).astype(jnp.float32)
            + factor[..., None] * gained
            - inputs * (factor**3 * mean)[..., None]
        ).astype(jnp.bfloat16)
        passed = pipe_back(grad)
        for at, source in enumerate(sources):
            first_out[source] = grad[at]
            second_blocks[source] = jnp.where(is_last, last_blocks[source], passed[at])

    second_grads = [None] * side
    for sources in CHUNKS:
        normed_grad = experts_of(1, sources, [second_blocks[source] for source in sources])
        for at, source in enumerate(sources):
            second_grads[source] = normed_grad[at].astype(jnp.bfloat16)

    first_grad = gather_features(first_out)
    upstream = jnp.where(is_last, upstream_last, pipe_back(first_grad)).astype(jnp.float32)
    gained = gather_features(second_grads).astype(jnp.float32) * gain
    inputs = saved_input[1].astype(jnp.float32)
    factor = inverse[1][:, None]
    second = (
        upstream
        + factor * gained
        - inputs * factor**3 * jnp.mean(inputs * gained, axis=-1, keepdims=True)
    ).astype(jnp.bfloat16)
    return (first_grad[None], second[None])


def solution(mesh):
    side = EXPERTS
    grid = Mesh(
        mesh.devices.reshape(mesh.shape["pipe"], side, mesh.shape["expert"] // side),
        ("pipe", "x", "z"),
    )
    expert = ("x", "z")
    return jax.shard_map(
        on_device,
        mesh=grid,
        in_specs=(
            P("pipe", expert, None),
            P(expert, None),
            P("pipe", None, expert, None),
            P("pipe", None),
            P("pipe", None, None),
            P("pipe", None, expert, None),
            P("pipe", expert, None, None),
            P("pipe", expert, None, None),
            P("pipe", expert, None, None),
            P("pipe", None, expert, None, None),
        ),
        out_specs=(P("pipe", expert, None), P("pipe", expert, None)),
        check_vma=False,
    )
```

```python
import jax
import jax.numpy as jnp
from jax import lax
from jax.experimental import pallas as pl
from jax.experimental.pallas import tpu as pltpu
from jax.sharding import Mesh
from jax.sharding import PartitionSpec as P

CAP = 72
EXPERTS = 4
CHUNKS = ((0, 1), (2, 3))

epsilon = 1e-06
route_scale = 2.5


def turned(value, axis, offset):
    if offset == 0:
        return value
    count = lax.axis_size(axis)
    return lax.ppermute(value, axis, [(i, (i + offset) % count) for i in range(count)])


def pick(stacked, index):
    return lax.dynamic_index_in_dim(stacked, index, 0, keepdims=False)


def split_in_two(value):
    high = value.astype(jnp.bfloat16)
    return high, (value - high.astype(jnp.float32)).astype(jnp.bfloat16)


def after(value, *earlier):
    anywhere = pl.BlockSpec(memory_space=pl.ANY)
    return pl.pallas_call(
        lambda *refs: None,
        out_shape=jax.ShapeDtypeStruct(value.shape, value.dtype),
        in_specs=[anywhere] * (1 + len(earlier)),
        out_specs=anywhere,
        input_output_aliases={0: 0},
        cost_estimate=pl.CostEstimate(flops=0, bytes_accessed=0, transcendentals=0),
    )(value, *earlier)


def activation(pieces, acts, spread, wave, at):
    depth, hidden = pieces[0].shape

    def kernel(p0, p1, p2, act_ref, spread_ref, out_ref):
        f32 = jnp.float32
        grad = p0[...].astype(f32) + p1[...].astype(f32) + p2[...].astype(f32)
        gate_pre = act_ref[:, :hidden].astype(f32)
        up_pre = act_ref[:, hidden:].astype(f32)
        sigmoid_g = jax.nn.sigmoid(gate_pre)
        up_grad = grad * (gate_pre * sigmoid_g)
        gate_grad = grad * up_pre * sigmoid_g * (1.0 + gate_pre * (1.0 - sigmoid_g))
        score = jnp.sum(up_grad * up_pre, axis=-1, keepdims=True).astype(jnp.bfloat16).astype(f32)
        out_ref[:, :hidden] = gate_grad.astype(jnp.bfloat16)
        out_ref[:, hidden : 2 * hidden] = up_grad.astype(jnp.bfloat16)
        term = score * spread_ref[...]
        high = term.astype(jnp.bfloat16).astype(f32)
        lane = lax.broadcasted_iota(jnp.int32, term.shape, 1)
        is_low = (lane >= EXPERTS) & (lane < 2 * EXPERTS)
        out_ref[:, 2 * hidden :] = jnp.where(is_low, term - high, high).astype(jnp.bfloat16)

    whole = pl.BlockSpec((depth, hidden), lambda i: (0, 0))
    return pl.pallas_call(
        kernel,
        grid=(1,),
        out_shape=jax.ShapeDtypeStruct((depth, 2 * hidden + 128), jnp.bfloat16),
        in_specs=[whole] * 3
        + [
            pl.BlockSpec((None, depth, 2 * hidden), lambda i: (wave, at, 0)),
            pl.BlockSpec((None, depth, 128), lambda i: (wave, at, 0)),
        ],
        out_specs=pl.BlockSpec((depth, 2 * hidden + 128), lambda i: (0, 0)),
        compiler_params=pltpu.CompilerParams(vmem_limit_bytes=40 * 2**20),
        cost_estimate=pl.CostEstimate(
            flops=30 * depth * hidden, bytes_accessed=18 * depth * hidden, transcendentals=depth * hidden
        ),
    )(*pieces, acts, spread)


def backward(own, above, far_gate, far_up, below, gate, up, tail, shift):
    depth, wide = own.shape
    part, hidden = gate.shape
    tile = 256
    side = 4

    def kernel(shift_ref, own_ref, above_ref, fg_ref, fu_ref, below_ref, g_ref, u_ref, t_ref, out_ref, held):
        @pl.when(pl.program_id(0) == 0)
        def _():
            held[:depth] = own_ref[...]
            held[depth : 2 * depth] = above_ref[...]
            held[2 * depth : 3 * depth, :hidden] = fg_ref[...]
            held[2 * depth : 3 * depth, hidden:] = fu_ref[...]
            held[3 * depth :] = below_ref[...]

        def times(first, last, ref):
            return lax.dot_general(
                held[:, first:last], ref[...], (((1,), (1,)), ((), ())), preferred_element_type=jnp.float32
            )

        rows = times(0, hidden, g_ref) + times(hidden, 2 * hidden, u_ref) + times(2 * hidden, wide, t_ref)
        rows = rows.astype(jnp.bfloat16)
        for at in range(side):
            out_ref[lax.rem(shift_ref[0] + at, side)] = rows[at * depth : (at + 1) * depth]

    def whole(array):
        return pl.BlockSpec(array.shape, lambda i, s: (0, 0))

    return pl.pallas_call(
        kernel,
        grid_spec=pltpu.PrefetchScalarGridSpec(
            num_scalar_prefetch=1,
            grid=(part // tile,),
            in_specs=[whole(own), whole(above), whole(far_gate), whole(far_up), whole(below)]
            + [
                pl.BlockSpec((tile, hidden), lambda i, s: (i, 0)),
                pl.BlockSpec((tile, hidden), lambda i, s: (i, 0)),
                pl.BlockSpec((tile, 128), lambda i, s: (i, 0)),
            ],
            out_specs=pl.BlockSpec((side, depth, tile), lambda i, s: (0, 0, i)),
            scratch_shapes=[pltpu.VMEM((side * depth, wide), jnp.bfloat16)],
        ),
        out_shape=jax.ShapeDtypeStruct((side, depth, part), jnp.bfloat16),
        compiler_params=pltpu.CompilerParams(vmem_limit_bytes=40 * 2**20),
        cost_estimate=pl.CostEstimate(
            flops=2 * side * depth * wide * part,
            bytes_accessed=2 * (wide * part + side * depth * (wide + part)),
            transcendentals=0,
        ),
    )(shift, own, above, far_gate, far_up, below, gate, up, tail)


def token_values(saved_input, gain, router, routes):
    waves, tokens, width = saved_input.shape
    flat = saved_input.reshape(waves * tokens, width)
    inputs = flat.astype(jnp.float32)
    inverse = lax.rsqrt(jnp.mean(inputs * inputs, axis=-1) + epsilon)
    scaled = gain[:, None] * router
    high = scaled.astype(jnp.bfloat16)
    rest = scaled - high.astype(jnp.float32)
    middle = rest.astype(jnp.bfloat16)
    low = (rest - middle.astype(jnp.float32)).astype(jnp.bfloat16)
    parts = jnp.dot(
        flat, jnp.concatenate([high, middle, low], axis=1), preferred_element_type=jnp.float32
    ).reshape(waves * tokens, 3, EXPERTS)
    logits = (parts[:, 0] + (parts[:, 1] + parts[:, 2])) * inverse[:, None]
    affinity = jax.nn.sigmoid(logits).reshape(waves, tokens, EXPERTS)
    routed = (routes[..., None] == jnp.arange(EXPERTS, dtype=jnp.int32)).astype(jnp.float32)
    chosen = jnp.sum(routed * affinity[:, :, None, :], axis=-1)
    total = jnp.sum(chosen, axis=-1, keepdims=True)
    weights = route_scale * chosen / total
    own = (1.0 - chosen) * (1.0 - chosen / total)
    other = -(chosen * (1.0 - chosen) / total)[:, :, ::-1]
    spread = own[..., None] * routed + other[..., None] * routed[:, :, ::-1]
    names = routes.reshape(waves, -1)
    count = names.shape[1]
    places = jnp.arange(count, dtype=jnp.int32)
    earlier = (names[:, :, None] == names[:, None, :]) & (places[None, :] < places[:, None])
    rank = jnp.sum(earlier.astype(jnp.int32), axis=-1)
    slots = (names * CAP + rank).reshape(waves, tokens, 2).astype(jnp.float32)
    packed = jnp.concatenate(
        [
            slots,
            weights,
            inverse.reshape(waves, tokens, 1),
            spread.reshape(waves, tokens, 2 * EXPERTS),
            jnp.zeros((waves, tokens, 3), jnp.float32),
        ],
        axis=-1,
    )
    return inverse.reshape(waves, tokens), jnp.swapaxes(packed, 1, 2)


def on_device(
    upstream_first,
    upstream_last,
    saved_input,
    norm_gain,
    router_weight,
    routes,
    w_gate,
    w_up,
    w_down,
    saved_preact,
):
    side = lax.axis_size("z")
    x_at, z_at = lax.axis_index("x"), lax.axis_index("z")
    pipe_count = lax.axis_size("pipe")
    is_last = lax.axis_index("pipe") == pipe_count - 1
    upstream_first, saved_input = upstream_first[0], saved_input[0]
    gain, router, routes = norm_gain[0], router_weight[0], routes[0]
    down_cols, preact = w_down[0, 0], saved_preact[0, :, 0]
    tokens, width = upstream_first.shape
    part = width // side
    hidden = down_cols.shape[0]

    def feature_block(value, index):
        return lax.dynamic_slice_in_dim(value, index % side * part, part, value.ndim - 1)

    def by_source(blocks):
        stacked = jnp.stack(blocks)
        return [pick(stacked, (z_at - source) % side) for source in range(side)]

    def everywhere(value, axis):
        value = value[None]
        for level in range(2):
            bit = 1 << level
            other = lax.ppermute(value, axis, [(i, i ^ bit) for i in range(side)])
            is_upper = lax.axis_index(axis) // bit % 2 == 1
            value = jnp.concatenate([jnp.where(is_upper, other, value), jnp.where(is_upper, value, other)])
        return value

    def turned_all(values, axis):
        return [turned(value, axis, off) for off, value in enumerate(values)]

    def spread_features(blocks):
        return by_source([turned(block, "z", off) for off, block in enumerate(blocks)])

    def gather_features(blocks, *earlier):
        stacked = jnp.stack(blocks)
        cut = [pick(stacked, (z_at + off) % side) for off in range(side)]
        if earlier:
            cut = [after(block, *earlier) for block in cut]
        whole = jnp.stack(turned_all(cut, "z"))
        return jnp.concatenate([pick(whole, (z_at - q) % side) for q in range(side)], axis=1)

    def pipe_back(value):
        return lax.ppermute(value, "pipe", [(i, i - 1) for i in range(1, pipe_count)])

    cut = [feature_block(upstream_first, z_at + off) for off in range(side)]
    first_blocks = turned_all(cut, "z")
    inverse, packed = token_values(saved_input, gain, router, after(routes, *cut))
    packed = after(everywhere(packed, "x"), first_blocks[1], first_blocks[3])
    facts = jnp.stack(by_source(turned_all([packed] * side, "z")))
    facts, senders = [lax.dynamic_index_in_dim(facts, at, 1, keepdims=False) for at in (x_at, z_at)]
    input_cut = [feature_block(saved_input[0], z_at + off) for off in range(side)]
    input_got = turned_all([after(block, *first_blocks[1:]) for block in input_cut], "z")
    input_blocks = by_source(input_got)
    first_blocks = by_source(first_blocks)
    last_blocks = []
    for off in range(side):
        value = feature_block(upstream_last, z_at + off)
        if off:
            stage = pipe_count - 1
            value = lax.ppermute(
                value,
                ("pipe", "z"),
                [(stage * side + i, stage * side + (i + off) % side) for i in range(side)],
            )
        last_blocks.append(value)
    last_got = last_blocks
    last_blocks = by_source(last_got)

    gain_block = feature_block(gain, z_at)
    router_block = lax.dynamic_slice_in_dim(router, z_at * part, part, 0)
    router_high, router_low = split_in_two(router_block)
    back_tail = jnp.concatenate(
        [
            router_high,
            router_high,
            router_low,
            jnp.zeros((part, 128 - 3 * EXPERTS), jnp.bfloat16),
        ],
        axis=1,
    )
    shift = lax.rem(z_at + side - x_at, side).astype(jnp.int32)[None]

    rows = jnp.arange(CAP, dtype=jnp.float32)[:, None]
    offsets = jnp.arange(side, dtype=jnp.int32)

    def matches(places, experts):
        first_slot = (experts * CAP).astype(jnp.float32)
        return places[..., None, :] - first_slot == rows

    def placing(wave):
        experts = ((x_at + offsets) % side)[:, None, None, None]
        both = matches(facts[:, wave, 0], experts) | matches(facts[:, wave, 1], experts)
        return both.astype(jnp.bfloat16)

    def weighing(wave):
        experts = ((x_at - offsets) % side)[:, None, None, None]
        return sum(
            jnp.where(matches(facts[:, wave, k], experts), facts[:, wave, 2 + k, None, :], 0.0)
            for k in range(2)
        ).astype(jnp.bfloat16)

    placed, weighed = [placing(0), placing(1)], [weighing(0), weighing(1)]

    match = jnp.concatenate(
        [matches(senders[:, :, k], x_at) for k in range(2)], axis=-1
    ).astype(jnp.bfloat16)
    fact = jnp.concatenate([senders[:, :, 5 + 4 * k : 9 + 4 * k] for k in range(2)], axis=-1)
    fact = jnp.concatenate([fact] * 3 + [jnp.zeros((side, 2, 128 - 3 * EXPERTS, fact.shape[-1]), fact.dtype)], axis=2)
    spreads = sum(
        jnp.einsum("swrt,swat->wsra", match, half, preferred_element_type=jnp.float32)
        for half in split_in_two(fact)
    ).reshape(2, side * CAP, 128)

    def dispatch(wave, sources, blocks):
        upstream = jnp.stack(blocks)
        sent = {}
        for off in (2, 1, 3, 0):
            place = placed[wave][off, sources[0] : sources[-1] + 1]
            sent[off] = jnp.einsum(
                "srt,stf->srf", place, upstream, preferred_element_type=jnp.bfloat16
            ).reshape(depth, part)
        return [sent[off] for off in range(side)]

    def partial_sums(arrived):
        partial = lax.dot_general(
            jnp.concatenate(arrived), down_cols, (((1,), (1,)), ((), ())), preferred_element_type=jnp.float32
        ).astype(jnp.bfloat16).reshape(side, depth, hidden)
        pieces = [pick(partial, (x_at - z_at - off) % side) for off in range(side)]
        half = hidden // 2
        upward, downward = turned(pieces[2][:, :half], "z", 1), turned(pieces[2][:, half:], "z", -1)

        def joined(first, second):
            return jnp.concatenate([first.astype(jnp.bfloat16), second.astype(jnp.bfloat16)], axis=1)

        f32 = jnp.float32
        up_sum = joined(pieces[1][:, :half].astype(f32) + upward.astype(f32), pieces[1][:, half:])
        down_sum = joined(pieces[3][:, :half], pieces[3][:, half:].astype(f32) + downward.astype(f32))
        return [pieces[0], turned(up_sum, "z", 1), turned(down_sum, "z", -1)]

    def gathered(grads):
        below, above = turned(grads, "z", 1), turned(grads, "z", -1)
        return [grads, above, below[:, :hidden], above[:, hidden:], below]

    def sent_on(parts):
        return [*parts[:2], turned(parts[2], "z", 1), turned(parts[3], "z", -1), parts[4]]

    def returned(back):
        return [turned(back[off], "x", off) for off in range(side)]

    def combine(wave, sources, rows):
        normed_grad = 0.0
        for off in (0, 1, 3, 2):
            normed_grad = normed_grad + jnp.einsum(
                "srt,srf->stf",
                weighed[wave][off, sources[0] : sources[-1] + 1],
                rows[off].reshape(len(sources), CAP, part),
                preferred_element_type=jnp.float32,
            )
        return normed_grad

    def finish_first(sources, normed_grad):
        gained = normed_grad * gain_block
        inputs = jnp.stack([input_blocks[source] for source in sources]).astype(jnp.float32)
        factor = jnp.stack([facts[source, 0, 4] for source in sources])
        share = jnp.sum(inputs * gained, axis=-1)
        mean = sum(turned(share, "z", off) for off in range(side)) / width
        return (
            jnp.stack([first_blocks[source] for source in sources]).astype(jnp.float32)
            + factor[..., None] * gained
            - inputs * (factor**3 * mean)[..., None]
        ).astype(jnp.bfloat16)

    depth = len(CHUNKS[0]) * CAP
    early, late = CHUNKS

    def middle(wave, sent_early, sent_late, first, offsets, then):
        if first:
            sent_early[0] = after(sent_early[0], *first)
        rows_late = turned_all(sent_late, "x")
        pieces = partial_sums(turned_all(sent_early, "x"))
        if offsets:
            pieces[0] = after(pieces[0], *[rows_late[off] for off in offsets])
        all_early = gathered(activation(pieces, preact, spreads, wave, 0))
        rows_late[0] = after(rows_late[0], all_early[2], all_early[3], *then)
        pieces = partial_sums(rows_late)
        back_early = backward(*sent_on(all_early), w_gate[0, 0], w_up[0, 0], back_tail, shift)
        pieces[0] = after(pieces[0], back_early)
        all_late = gathered(activation(pieces, preact, spreads, wave, 1))
        back_late = backward(*sent_on(all_late), w_gate[0, 0], w_up[0, 0], back_tail, shift)
        rows_early, rows_late = returned(back_early), returned(back_late)
        rows_early[0] = after(rows_early[0], rows_late[0])
        return rows_early, rows_late, back_late

    sent_early = dispatch(0, early, [first_blocks[source] for source in early])
    sent_late = dispatch(0, late, [first_blocks[source] for source in late])
    rows_early, rows_late, _ = middle(
        0, sent_early, sent_late, [*sent_late, *input_got[1:]], (1, 2, 3), last_got[1:]
    )
    second_blocks, first_out = [None] * side, [None] * side
    second_sent = []
    for sources, rows in ((early, rows_early), (late, rows_late)):
        if second_sent:
            rows[0] = after(rows[0], *second_sent[0])
        grad = finish_first(sources, combine(0, sources, rows))
        passed = pipe_back(grad)
        for at, source in enumerate(sources):
            first_out[source] = grad[at]
            second_blocks[source] = jnp.where(is_last, last_blocks[source], passed[at])
        second_sent.append(dispatch(1, sources, [second_blocks[source] for source in sources]))

    rows_early, rows_late, back_late = middle(1, *second_sent, [], (), [])
    first_grad = gather_features(first_out, back_late)

    second_grads = [None] * side
    for sources, rows in ((early, rows_early), (late, rows_late)):
        normed_grad = combine(1, sources, rows)
        for at, source in enumerate(sources):
            second_grads[source] = normed_grad[at].astype(jnp.bfloat16)

    upstream = jnp.where(is_last, upstream_last, pipe_back(first_grad)).astype(jnp.float32)
    gained = gather_features(second_grads).astype(jnp.float32) * gain
    inputs = saved_input[1].astype(jnp.float32)
    factor = inverse[1][:, None]
    second = (
        upstream
        + factor * gained
        - inputs * factor**3 * jnp.mean(inputs * gained, axis=-1, keepdims=True)
    ).astype(jnp.bfloat16)
    return (first_grad[None], second[None])


def solution(mesh):
    side = EXPERTS
    grid = Mesh(
        mesh.devices.reshape(mesh.shape["pipe"], side, mesh.shape["expert"] // side),
        ("pipe", "x", "z"),
    )
    expert = ("x", "z")
    return jax.shard_map(
        on_device,
        mesh=grid,
        in_specs=(
            P("pipe", expert, None),
            P(expert, None),
            P("pipe", None, expert, None),
            P("pipe", None),
            P("pipe", None, None),
            P("pipe", None, expert, None),
            P("pipe", expert, None, None),
            P("pipe", expert, None, None),
            P("pipe", expert, None, None),
            P("pipe", None, expert, None, None),
        ),
        out_specs=(P("pipe", expert, None), P("pipe", expert, None)),
        check_vma=False,
    )
```

```python
import jax
import jax.numpy as jnp
from jax import lax
from jax.experimental import pallas as pl
from jax.experimental.pallas import tpu as pltpu
from jax.sharding import Mesh
from jax.sharding import PartitionSpec as P

CAP = 72
EXPERTS = 4
CHUNKS = ((0, 1), (2, 3))

epsilon = 1e-06
route_scale = 2.5


def turned(value, axis, offset):
    if offset == 0:
        return value
    count = lax.axis_size(axis)
    return lax.ppermute(value, axis, [(i, (i + offset) % count) for i in range(count)])


def pick(stacked, index):
    return lax.dynamic_index_in_dim(stacked, index, 0, keepdims=False)


def split_in_two(value):
    high = value.astype(jnp.bfloat16)
    return high, (value - high.astype(jnp.float32)).astype(jnp.bfloat16)


def after(value, *earlier):
    anywhere = pl.BlockSpec(memory_space=pl.ANY)
    return pl.pallas_call(
        lambda *refs: None,
        out_shape=jax.ShapeDtypeStruct(value.shape, value.dtype),
        in_specs=[anywhere] * (1 + len(earlier)),
        out_specs=anywhere,
        input_output_aliases={0: 0},
        cost_estimate=pl.CostEstimate(flops=0, bytes_accessed=0, transcendentals=0),
    )(value, *earlier)


def activation(pieces, acts, spread, wave, at):
    depth, hidden = pieces[0].shape

    def kernel(p0, p1, p2, act_ref, spread_ref, out_ref):
        f32 = jnp.float32
        grad = p0[...].astype(f32) + p1[...].astype(f32) + p2[...].astype(f32)
        gate_pre = act_ref[:, :hidden].astype(f32)
        up_pre = act_ref[:, hidden:].astype(f32)
        sigmoid_g = jax.nn.sigmoid(gate_pre)
        up_grad = grad * (gate_pre * sigmoid_g)
        gate_grad = grad * up_pre * sigmoid_g * (1.0 + gate_pre * (1.0 - sigmoid_g))
        score = jnp.sum(up_grad * up_pre, axis=-1, keepdims=True).astype(jnp.bfloat16).astype(f32)
        out_ref[:, :hidden] = gate_grad.astype(jnp.bfloat16)
        out_ref[:, hidden : 2 * hidden] = up_grad.astype(jnp.bfloat16)
        term = score * spread_ref[...]
        high = term.astype(jnp.bfloat16).astype(f32)
        lane = lax.broadcasted_iota(jnp.int32, term.shape, 1)
        is_low = (lane >= EXPERTS) & (lane < 2 * EXPERTS)
        out_ref[:, 2 * hidden :] = jnp.where(is_low, term - high, high).astype(jnp.bfloat16)

    whole = pl.BlockSpec((depth, hidden), lambda i: (0, 0))
    return pl.pallas_call(
        kernel,
        grid=(1,),
        out_shape=jax.ShapeDtypeStruct((depth, 2 * hidden + 128), jnp.bfloat16),
        in_specs=[whole] * 3
        + [
            pl.BlockSpec((None, depth, 2 * hidden), lambda i: (wave, at, 0)),
            pl.BlockSpec((None, depth, 128), lambda i: (wave, at, 0)),
        ],
        out_specs=pl.BlockSpec((depth, 2 * hidden + 128), lambda i: (0, 0)),
        compiler_params=pltpu.CompilerParams(vmem_limit_bytes=40 * 2**20),
        cost_estimate=pl.CostEstimate(
            flops=30 * depth * hidden, bytes_accessed=18 * depth * hidden, transcendentals=depth * hidden
        ),
    )(*pieces, acts, spread)


def backward(own, above, far_gate, far_up, below, gate, up, tail, shift):
    depth, wide = own.shape
    part, hidden = gate.shape
    tile = 256
    side = 4

    def kernel(shift_ref, own_ref, above_ref, fg_ref, fu_ref, below_ref, g_ref, u_ref, t_ref, out_ref, held):
        @pl.when(pl.program_id(0) == 0)
        def _():
            held[:depth] = own_ref[...]
            held[depth : 2 * depth] = above_ref[...]
            held[2 * depth : 3 * depth, :hidden] = fg_ref[...]
            held[2 * depth : 3 * depth, hidden:] = fu_ref[...]
            held[3 * depth :] = below_ref[...]

        def times(first, last, ref):
            return lax.dot_general(
                held[:, first:last], ref[...], (((1,), (1,)), ((), ())), preferred_element_type=jnp.float32
            )

        rows = times(0, hidden, g_ref) + times(hidden, 2 * hidden, u_ref) + times(2 * hidden, wide, t_ref)
        rows = rows.astype(jnp.bfloat16)
        for at in range(side):
            out_ref[lax.rem(shift_ref[0] + at, side)] = rows[at * depth : (at + 1) * depth]

    def whole(array):
        return pl.BlockSpec(array.shape, lambda i, s: (0, 0))

    return pl.pallas_call(
        kernel,
        grid_spec=pltpu.PrefetchScalarGridSpec(
            num_scalar_prefetch=1,
            grid=(part // tile,),
            in_specs=[whole(own), whole(above), whole(far_gate), whole(far_up), whole(below)]
            + [
                pl.BlockSpec((tile, hidden), lambda i, s: (i, 0)),
                pl.BlockSpec((tile, hidden), lambda i, s: (i, 0)),
                pl.BlockSpec((tile, 128), lambda i, s: (i, 0)),
            ],
            out_specs=pl.BlockSpec((side, depth, tile), lambda i, s: (0, 0, i)),
            scratch_shapes=[pltpu.VMEM((side * depth, wide), jnp.bfloat16)],
        ),
        out_shape=jax.ShapeDtypeStruct((side, depth, part), jnp.bfloat16),
        compiler_params=pltpu.CompilerParams(vmem_limit_bytes=40 * 2**20),
        cost_estimate=pl.CostEstimate(
            flops=2 * side * depth * wide * part,
            bytes_accessed=2 * (wide * part + side * depth * (wide + part)),
            transcendentals=0,
        ),
    )(shift, own, above, far_gate, far_up, below, gate, up, tail)


def token_values(saved_input, gain, router, routes):
    waves, tokens, width = saved_input.shape
    flat = saved_input.reshape(waves * tokens, width)
    inputs = flat.astype(jnp.float32)
    inverse = lax.rsqrt(jnp.mean(inputs * inputs, axis=-1) + epsilon)
    scaled = gain[:, None] * router
    high = scaled.astype(jnp.bfloat16)
    rest = scaled - high.astype(jnp.float32)
    middle = rest.astype(jnp.bfloat16)
    low = (rest - middle.astype(jnp.float32)).astype(jnp.bfloat16)
    parts = jnp.dot(
        flat, jnp.concatenate([high, middle, low], axis=1), preferred_element_type=jnp.float32
    ).reshape(waves * tokens, 3, EXPERTS)
    logits = (parts[:, 0] + (parts[:, 1] + parts[:, 2])) * inverse[:, None]
    affinity = jax.nn.sigmoid(logits).reshape(waves, tokens, EXPERTS)
    routed = (routes[..., None] == jnp.arange(EXPERTS, dtype=jnp.int32)).astype(jnp.float32)
    chosen = jnp.sum(routed * affinity[:, :, None, :], axis=-1)
    total = jnp.sum(chosen, axis=-1, keepdims=True)
    weights = route_scale * chosen / total
    own = (1.0 - chosen) * (1.0 - chosen / total)
    other = -(chosen * (1.0 - chosen) / total)[:, :, ::-1]
    spread = own[..., None] * routed + other[..., None] * routed[:, :, ::-1]
    names = routes.reshape(waves, -1)
    count = names.shape[1]
    places = jnp.arange(count, dtype=jnp.int32)
    earlier = (names[:, :, None] == names[:, None, :]) & (places[None, :] < places[:, None])
    rank = jnp.sum(earlier.astype(jnp.int32), axis=-1)
    slots = (names * CAP + rank).reshape(waves, tokens, 2).astype(jnp.float32)
    packed = jnp.concatenate(
        [
            slots,
            weights,
            inverse.reshape(waves, tokens, 1),
            spread.reshape(waves, tokens, 2 * EXPERTS),
            jnp.zeros((waves, tokens, 3), jnp.float32),
        ],
        axis=-1,
    )
    return inverse.reshape(waves, tokens), jnp.swapaxes(packed, 1, 2)


def on_device(
    upstream_first,
    upstream_last,
    saved_input,
    norm_gain,
    router_weight,
    routes,
    w_gate,
    w_up,
    w_down,
    saved_preact,
):
    side = lax.axis_size("z")
    x_at, z_at = lax.axis_index("x"), lax.axis_index("z")
    pipe_count = lax.axis_size("pipe")
    is_last = lax.axis_index("pipe") == pipe_count - 1
    upstream_first, saved_input = upstream_first[0], saved_input[0]
    gain, router, routes = norm_gain[0], router_weight[0], routes[0]
    down_cols, preact = w_down[0, 0], saved_preact[0, :, 0]
    tokens, width = upstream_first.shape
    part = width // side
    hidden = down_cols.shape[0]

    def feature_block(value, index):
        return lax.dynamic_slice_in_dim(value, index % side * part, part, value.ndim - 1)

    def by_source(blocks):
        stacked = jnp.stack(blocks)
        return [pick(stacked, (z_at - source) % side) for source in range(side)]

    def everywhere(value, axis):
        value = value[None]
        for level in range(2):
            bit = 1 << level
            other = lax.ppermute(value, axis, [(i, i ^ bit) for i in range(side)])
            is_upper = lax.axis_index(axis) // bit % 2 == 1
            value = jnp.concatenate([jnp.where(is_upper, other, value), jnp.where(is_upper, value, other)])
        return value

    def turned_all(values, axis):
        return [turned(value, axis, off) for off, value in enumerate(values)]

    def spread_features(blocks):
        return by_source([turned(block, "z", off) for off, block in enumerate(blocks)])

    def gather_features(blocks, *earlier):
        stacked = jnp.stack(blocks)
        cut = [pick(stacked, (z_at + off) % side) for off in range(side)]
        if earlier:
            cut = [after(block, *earlier) for block in cut]
        whole = jnp.stack(turned_all(cut, "z"))
        return jnp.concatenate([pick(whole, (z_at - q) % side) for q in range(side)], axis=1)

    def pipe_back(value):
        return lax.ppermute(value, "pipe", [(i, i - 1) for i in range(1, pipe_count)])

    cut = [feature_block(upstream_first, z_at + off) for off in range(side)]
    first_blocks = turned_all(cut, "z")
    inverse, packed = token_values(saved_input, gain, router, after(routes, *cut))
    packed = after(everywhere(packed, "x"), first_blocks[1], first_blocks[3])
    facts = jnp.stack(by_source(turned_all([packed] * side, "z")))
    facts, senders = [lax.dynamic_index_in_dim(facts, at, 1, keepdims=False) for at in (x_at, z_at)]
    input_cut = [feature_block(saved_input[0], z_at + off) for off in range(side)]
    input_got = turned_all([after(block, *first_blocks[1:]) for block in input_cut], "z")
    input_blocks = by_source(input_got)
    first_blocks = by_source(first_blocks)
    last_blocks = []
    for off in range(side):
        value = feature_block(upstream_last, z_at + off)
        if off:
            stage = pipe_count - 1
            value = lax.ppermute(
                value,
                ("pipe", "z"),
                [(stage * side + i, stage * side + (i + off) % side) for i in range(side)],
            )
        last_blocks.append(value)
    last_got = last_blocks
    last_blocks = by_source(last_got)

    gain_block = feature_block(gain, z_at)
    router_block = lax.dynamic_slice_in_dim(router, z_at * part, part, 0)
    router_high, router_low = split_in_two(router_block)
    back_tail = jnp.concatenate(
        [
            router_high,
            router_high,
            router_low,
            jnp.zeros((part, 128 - 3 * EXPERTS), jnp.bfloat16),
        ],
        axis=1,
    )
    shift = lax.rem(z_at + side - x_at, side).astype(jnp.int32)[None]

    rows = jnp.arange(CAP, dtype=jnp.float32)[:, None]
    offsets = jnp.arange(side, dtype=jnp.int32)

    def matches(places, experts):
        first_slot = (experts * CAP).astype(jnp.float32)
        return places[..., None, :] - first_slot == rows

    def placing(wave):
        experts = ((x_at + offsets) % side)[:, None, None, None]
        both = matches(facts[:, wave, 0], experts) | matches(facts[:, wave, 1], experts)
        return both.astype(jnp.bfloat16)

    def weighing(wave):
        experts = ((x_at - offsets) % side)[:, None, None, None]
        return sum(
            jnp.where(matches(facts[:, wave, k], experts), facts[:, wave, 2 + k, None, :], 0.0)
            for k in range(2)
        ).astype(jnp.bfloat16)

    placed, weighed = [placing(0), placing(1)], [weighing(0), weighing(1)]

    match = jnp.concatenate(
        [matches(senders[:, :, k], x_at) for k in range(2)], axis=-1
    ).astype(jnp.bfloat16)
    fact = jnp.concatenate([senders[:, :, 5 + 4 * k : 9 + 4 * k] for k in range(2)], axis=-1)
    fact = jnp.concatenate([fact] * 3 + [jnp.zeros((side, 2, 128 - 3 * EXPERTS, fact.shape[-1]), fact.dtype)], axis=2)
    spreads = sum(
        jnp.einsum("swrt,swat->wsra", match, half, preferred_element_type=jnp.float32)
        for half in split_in_two(fact)
    ).reshape(2, side * CAP, 128)

    def dispatch(wave, sources, blocks):
        upstream = jnp.stack(blocks)
        sent = {}
        for off in (2, 1, 3, 0):
            place = placed[wave][off, sources[0] : sources[-1] + 1]
            sent[off] = jnp.einsum(
                "srt,stf->srf", place, upstream, preferred_element_type=jnp.bfloat16
            ).reshape(depth, part)
        return [sent[off] for off in range(side)]

    def partial_sums(arrived):
        partial = lax.dot_general(
            jnp.concatenate(arrived), down_cols, (((1,), (1,)), ((), ())), preferred_element_type=jnp.float32
        ).astype(jnp.bfloat16).reshape(side, depth, hidden)
        pieces = [pick(partial, (x_at - z_at - off) % side) for off in range(side)]
        half = hidden // 2
        upward, downward = turned(pieces[2][:, :half], "z", 1), turned(pieces[2][:, half:], "z", -1)

        def joined(first, second):
            return jnp.concatenate([first.astype(jnp.bfloat16), second.astype(jnp.bfloat16)], axis=1)

        f32 = jnp.float32
        up_sum = joined(pieces[1][:, :half].astype(f32) + upward.astype(f32), pieces[1][:, half:])
        down_sum = joined(pieces[3][:, :half], pieces[3][:, half:].astype(f32) + downward.astype(f32))
        return [pieces[0], turned(up_sum, "z", 1), turned(down_sum, "z", -1)]

    def gathered(grads):
        below, above = turned(grads, "z", 1), turned(grads, "z", -1)
        return [grads, above, below[:, :hidden], above[:, hidden:], below]

    def sent_on(parts):
        return [*parts[:2], turned(parts[2], "z", 1), turned(parts[3], "z", -1), parts[4]]

    def returned(back):
        return [turned(back[off], "x", off) for off in range(side)]

    def combine(wave, sources, rows):
        normed_grad = 0.0
        for off in (0, 1, 3, 2):
            normed_grad = normed_grad + jnp.einsum(
                "srt,srf->stf",
                weighed[wave][off, sources[0] : sources[-1] + 1],
                rows[off].reshape(len(sources), CAP, part),
                preferred_element_type=jnp.float32,
            )
        return normed_grad

    def finish_first(sources, normed_grad):
        gained = normed_grad * gain_block
        inputs = jnp.stack([input_blocks[source] for source in sources]).astype(jnp.float32)
        factor = jnp.stack([facts[source, 0, 4] for source in sources])
        share = jnp.sum(inputs * gained, axis=-1)
        mean = sum(turned(share, "z", off) for off in range(side)) / width
        return (
            jnp.stack([first_blocks[source] for source in sources]).astype(jnp.float32)
            + factor[..., None] * gained
            - inputs * (factor**3 * mean)[..., None]
        ).astype(jnp.bfloat16)

    depth = len(CHUNKS[0]) * CAP
    early, late = CHUNKS

    def middle(wave, sent_early, sent_late, first, offsets, then):
        if first:
            sent_early[0] = after(sent_early[0], *first)
        rows_late = turned_all(sent_late, "x")
        pieces = partial_sums(turned_all(sent_early, "x"))
        if offsets:
            pieces[0] = after(pieces[0], *[rows_late[off] for off in offsets])
        all_early = gathered(activation(pieces, preact, spreads, wave, 0))
        rows_late[0] = after(rows_late[0], all_early[2], all_early[3], *then)
        pieces = partial_sums(rows_late)
        back_early = backward(*sent_on(all_early), w_gate[0, 0], w_up[0, 0], back_tail, shift)
        all_late = gathered(activation(pieces, preact, spreads, wave, 1))
        back_late = backward(*sent_on(all_late), w_gate[0, 0], w_up[0, 0], back_tail, shift)
        rows_early, rows_late = returned(back_early), returned(back_late)
        rows_early[0] = after(rows_early[0], rows_late[0])
        return rows_early, rows_late, back_late

    sent_early = dispatch(0, early, [first_blocks[source] for source in early])
    sent_late = dispatch(0, late, [first_blocks[source] for source in late])
    rows_early, rows_late, _ = middle(
        0, sent_early, sent_late, [*sent_late, *input_got[1:]], (1, 2, 3), last_got[1:]
    )
    second_blocks, first_out = [None] * side, [None] * side
    second_sent = []
    for sources, rows in ((early, rows_early), (late, rows_late)):
        if second_sent:
            rows[0] = after(rows[0], *second_sent[0])
        grad = finish_first(sources, combine(0, sources, rows))
        passed = pipe_back(grad)
        for at, source in enumerate(sources):
            first_out[source] = grad[at]
            second_blocks[source] = jnp.where(is_last, last_blocks[source], passed[at])
        second_sent.append(dispatch(1, sources, [second_blocks[source] for source in sources]))

    rows_early, rows_late, back_late = middle(1, *second_sent, [], (1, 3), [])
    first_grad = gather_features(first_out, back_late)

    second_grads = [None] * side
    for sources, rows in ((early, rows_early), (late, rows_late)):
        normed_grad = combine(1, sources, rows)
        for at, source in enumerate(sources):
            second_grads[source] = normed_grad[at].astype(jnp.bfloat16)

    upstream = jnp.where(is_last, upstream_last, pipe_back(first_grad)).astype(jnp.float32)
    gained = gather_features(second_grads).astype(jnp.float32) * gain
    inputs = saved_input[1].astype(jnp.float32)
    factor = inverse[1][:, None]
    second = (
        upstream
        + factor * gained
        - inputs * factor**3 * jnp.mean(inputs * gained, axis=-1, keepdims=True)
    ).astype(jnp.bfloat16)
    return (first_grad[None], second[None])


def solution(mesh):
    side = EXPERTS
    grid = Mesh(
        mesh.devices.reshape(mesh.shape["pipe"], side, mesh.shape["expert"] // side),
        ("pipe", "x", "z"),
    )
    expert = ("x", "z")
    return jax.shard_map(
        on_device,
        mesh=grid,
        in_specs=(
            P("pipe", expert, None),
            P(expert, None),
            P("pipe", None, expert, None),
            P("pipe", None),
            P("pipe", None, None),
            P("pipe", None, expert, None),
            P("pipe", expert, None, None),
            P("pipe", expert, None, None),
            P("pipe", expert, None, None),
            P("pipe", None, expert, None, None),
        ),
        out_specs=(P("pipe", expert, None), P("pipe", expert, None)),
        check_vma=False,
    )
```
